32 devices in a mesh: outer: 4 (over z), inner: 2 (over core), heads: 4 (over y, x).
Axes of the slice: x: 2, y: 2, z: 4, core: 2. Of those that a mesh axis runs over, the one named last changes fastest.
Arguments:
- lin_query: bfloat16 [1024, 8192], P(('outer', 'inner'), 'heads'), may hold values from -6 to 6
- lin_key: bfloat16 [1024, 8192], P(('outer', 'inner'), 'heads'), may hold values from -6 to 6
- lin_value: bfloat16 [1024, 8192], P(('outer', 'inner'), 'heads'), may hold values from -18 to 18
- gate_input: bfloat16 [1024, 8192], P(('outer', 'inner'), 'heads'), may hold values from -6 to 6
- norm_gain: bfloat16 [8192], P('heads'), may hold values from 0.099609375 to 1.8984375
- segment_ids: int32 [1024], P(('outer', 'inner')), may hold values from 0 to 4, never falling along the last dimension, each value on 1 to 384 neighbouring positions
- soft_query: bfloat16 [1024, 8192], P(('outer', 'inner'), 'heads'), may hold values from -10 to 10
- soft_key: bfloat16 [1024, 8192], P(('outer', 'inner'), 'heads'), may hold values from -4 to 4
Outputs:
- linear_out: bfloat16 [1024, 8192], P(('outer', 'inner'), 'heads')
- attended: bfloat16 [1024, 8192], P(('outer', 'inner'), 'heads')
The draws below stay inside these ranges and needn't reach their ends.
Inputs may be any that keep to these rules, and one draw needn't show every extreme that they name: `segment_ids`: numbers never fall along the sequence, every number from 0 to 4 is used, and a document has at most 384 tokens.
All inputs are finite; a program needn't handle non-finite values.
Results may differ from the reference program's by a relative error of at most 0.0062.
Values may be sent and summed in bfloat16 or wider, within the bound.
No kernel may reach another device: no remote copies, remote signals or barrier semaphores. Data moves between devices by JAX's collectives and lax.ppermute only.
A program may use at most 64 MiB of HBM per device.

```python
import math
import jax
import jax.numpy as jnp
import numpy as np
from jax import lax

H = 64
DH = 128
TOK_DEV = 128
SPAN = 3
SEQ = 1024
MOSTDOC = 384
DOCS = 5


def draw_lin_value(key, part):
    ramp = jnp.arange(H, dtype=jnp.float32) / (H - 1)
    base = jnp.clip(jax.random.normal(key, (SEQ, H, DH), jnp.float32), -4.0, 4.0)
    scales = 3.0 ** ramp
    return (base * scales[None, :, None]).reshape(SEQ, H * DH).astype(jnp.bfloat16)


def draw_soft_key(key, part):
    base = jnp.clip(jax.random.normal(jax.random.fold_in(key, 1), (SEQ, H, DH), jnp.float32), -4.0, 4.0)
    return base.reshape(SEQ, H * DH).astype(jnp.bfloat16)


def draw_soft_query(key, part):
    base = jnp.clip(jax.random.normal(jax.random.fold_in(key, 2), (SEQ, H, DH), jnp.float32), -4.0, 4.0)
    return base.reshape(SEQ, H * DH).astype(jnp.bfloat16)


def block_scale(own_key, shape, pieces, low, high):
    gain, own = 1.0, jax.random.fold_in(own_key, 6)
    for axis_at, parts in pieces:
        draws = jnp.exp(jax.random.uniform(jax.random.fold_in(own, axis_at), (parts,), jnp.float32, low / len(pieces), high / len(pieces)))
        gain = gain * jnp.repeat(draws, shape[axis_at] // parts).reshape([-1 if axis == axis_at else 1 for axis in range(len(shape))])
    return gain


def split_up(amount, total, reach, slope):
    portions = [(1 << 20) // math.isqrt(standing ** slope) + 1 for standing in range(2, amount + 1)]
    spare, holding = total - reach - (amount - 1), [1] * (amount - 1)
    while spare > 0:
        free = [i for i in range(amount - 1) if holding[i] < reach]
        mass, left = sum([portions[i] for i in free]), spare
        for i in free:
            addition = min(reach - holding[i], max(1, left * portions[i] // mass), spare)
            holding[i] = holding[i] + addition
            spare = spare - addition
    return np.array([reach] + holding)


def uneven(rng, count, total, most, lean):
    if count == 2:
        one = jax.random.randint(rng, (), max(1, total - most), min(most, total - 1) + 1)
        return jnp.stack([one, total - one])
    tallies = jnp.asarray(split_up(count, total, most, lean), jnp.int32)
    pairs = (count - 1) // 2
    donor, sink = tallies[1:1 + 2 * pairs:2], tallies[2:2 + 2 * pairs:2]
    room = jnp.minimum(donor - 1, most - sink)
    passed = jax.random.randint(jax.random.fold_in(rng, 1), (pairs,), 0, 1 << 20) % (room + 1)
    tallies = tallies.at[1:1 + 2 * pairs:2].set(donor - passed).at[2:2 + 2 * pairs:2].set(sink + passed)
    return tallies[jax.random.permutation(jax.random.fold_in(rng, 2), count)]


def noise(rng, extent, width, reach, cuts=(), kind=jnp.bfloat16):
    result = jax.random.normal(rng, extent, jnp.float32) * width
    if len(cuts) > 0:
        result = block_scale(rng, extent, cuts, -0.22, 0.18) * result
    return jnp.clip(result, min=-reach, max=reach).astype(kind)


def setup_inputs(seed: int = 0) -> dict:
    key_list = jax.random.split(jax.random.key(seed), 9)
    lin_query = noise(key_list[0], (SEQ, H * DH), 1.0, 6.0, ((0, 8), (1, 4)))
    lin_key = noise(key_list[1], (SEQ, H * DH), 1.0, 6.0, ((0, 8), (1, 4)))
    lin_value = draw_lin_value(jax.random.fold_in(key_list[8], 71), 0)
    gate_input = noise(key_list[3], (SEQ, H * DH), 1.0, 6.0, ((0, 8), (1, 4)))
    norm_gain = jnp.clip(1.0 + 0.18 * jax.random.normal(key_list[4], (H * DH,), jnp.float32), 0.099609375, 1.8984375).astype(jnp.bfloat16)
    segment_ids = jnp.searchsorted(jnp.cumsum(uneven(key_list[5], DOCS, SEQ, MOSTDOC, 2)), jnp.arange(SEQ), side="right").astype(jnp.int32)
    soft_query = draw_soft_query(jax.random.fold_in(key_list[8], 71), 0)
    soft_key = draw_soft_key(jax.random.fold_in(key_list[8], 71), 0)
    return {"lin_query": lin_query, "lin_key": lin_key, "lin_value": lin_value, "gate_input": gate_input, "norm_gain": norm_gain, "segment_ids": segment_ids, "soft_query": soft_query, "soft_key": soft_key}


def reference(lin_query, lin_key, lin_value, gate_input, norm_gain, segment_ids, soft_query, soft_key):
    block_count = SEQ // TOK_DEV
    head_shape = (block_count, TOK_DEV, H, DH)
    queries = lin_query.reshape(head_shape)
    key_blocks = lin_key.reshape(head_shape)
    value_blocks = lin_value.reshape(head_shape)
    gate_blocks = gate_input.reshape(head_shape)
    documents = segment_ids.astype(jnp.int32).reshape(block_count, TOK_DEV)
    gain_cols = norm_gain.astype(jnp.float32).reshape(1, H, DH)
    token_index = jnp.arange(TOK_DEV, dtype=jnp.int32)
    causal = token_index[:, None] >= token_index[None, :]

    def linear_block(carried_in, block_item):
        carried_state, carried_doc = carried_in
        q_rows, k_rows, v_rows, g_rows, doc_rows = block_item
        q_float = q_rows.astype(jnp.float32)
        k_float = k_rows.astype(jnp.float32)
        v_float = v_rows.astype(jnp.float32)
        raw_scores = jnp.einsum('thd,shd->hts', q_float, k_float)
        visible = causal & (doc_rows[:, None] == doc_rows[None, :])
        intra_weights = lax.optimization_barrier(jnp.where(visible[None], raw_scores, 0.0).astype(jnp.bfloat16)).astype(jnp.float32)
        intra_part = jnp.einsum('hts,shd->thd', intra_weights, v_float)
        carried_part = jnp.einsum('thd,hde->the', q_float, carried_state, precision=lax.Precision.HIGHEST)
        mixed = intra_part + jnp.where((doc_rows == carried_doc)[:, None, None], carried_part, 0.0)
        mean_square = lax.optimization_barrier(jnp.mean(mixed * mixed, axis=(1, 2)))
        linear_rows = (mixed * lax.rsqrt(mean_square + 1e-05)[:, None, None] * gain_cols * jax.nn.sigmoid(g_rows.astype(jnp.float32))).astype(jnp.bfloat16)
        final_doc = doc_rows[-1]
        kept = jnp.where((doc_rows == final_doc)[:, None, None], k_float, 0.0)
        block_state = jnp.einsum('thd,the->hde', kept, v_float)
        next_state = block_state + jnp.where(carried_doc == final_doc, carried_state, 0.0)
        return ((next_state, final_doc), linear_rows)
    start_state = (jnp.zeros((H, DH, DH), jnp.float32), jnp.array(-1, jnp.int32))
    _, linear_blocks = lax.scan(linear_block, start_state, (queries, key_blocks, value_blocks, gate_blocks, documents))
    linear_out = linear_blocks.reshape(SEQ, H * DH)
    margin = SPAN * TOK_DEV
    padded_keys = jnp.concatenate([jnp.zeros((margin, H, DH), soft_key.dtype), soft_key.reshape(SEQ, H, DH)], axis=0)
    padded_values = jnp.concatenate([jnp.zeros((margin, H, DH), linear_out.dtype), linear_out.reshape(SEQ, H, DH)], axis=0)
    padded_docs = jnp.concatenate([jnp.full((margin,), -1, jnp.int32), segment_ids.astype(jnp.int32)])
    key_positions = jnp.arange(SEQ + margin, dtype=jnp.int32) - margin
    soft_rows = soft_query.reshape(SEQ, H, DH)
    all_docs = segment_ids.astype(jnp.int32)

    def attend(block):
        first = (block * TOK_DEV).astype(jnp.int32)
        key_rows = lax.dynamic_slice_in_dim(padded_keys, first, margin + TOK_DEV, 0)
        value_rows = lax.dynamic_slice_in_dim(padded_values, first, margin + TOK_DEV, 0)
        key_docs = lax.dynamic_slice_in_dim(padded_docs, first, margin + TOK_DEV, 0)
        key_pos = lax.dynamic_slice_in_dim(key_positions, first, margin + TOK_DEV, 0)
        query_rows = lax.dynamic_slice_in_dim(soft_rows, first, TOK_DEV, 0)
        query_docs = lax.dynamic_slice_in_dim(all_docs, first, TOK_DEV, 0)
        query_positions = first + token_index
        scores = jnp.einsum('thd,shd->hts', query_rows.astype(jnp.float32), key_rows.astype(jnp.float32)) * (1.0 / math.sqrt(DH))
        visible = (query_docs[:, None] == key_docs[None, :]) & (key_pos[None, :] <= query_positions[:, None])
        masked = jnp.where(visible[None], scores, -jnp.inf)
        row_top = lax.optimization_barrier(jnp.max(masked, axis=2, keepdims=True))
        exponent = jnp.where(visible[None], jnp.exp(masked - row_top), 0.0)
        soft_weights = lax.optimization_barrier((exponent / lax.optimization_barrier(jnp.sum(exponent, axis=2, keepdims=True))).astype(jnp.bfloat16)).astype(jnp.float32)
        return jnp.einsum('hts,shd->thd', soft_weights, value_rows.astype(jnp.float32)).astype(jnp.bfloat16)
    attended = lax.map(attend, jnp.arange(block_count, dtype=jnp.int32)).reshape(SEQ, H * DH)
    return (linear_out, attended)
```

```python
import functools
import math

import jax
import jax.numpy as jnp
from jax import lax
from jax.experimental import pallas as pl
from jax.experimental.pallas import tpu as pltpu
from jax.sharding import PartitionSpec as P

DH = 128
PAD = 16
F32 = jnp.float32
BF16 = jnp.bfloat16
VMEM_LIMIT = 32 * 1024 * 1024


def dot(a, b, dims=((1,), (0,))):
    return lax.dot_general(a, b, (dims, ((), ())), preferred_element_type=F32)


def column(row):
    n = row.shape[1]
    parts = [
        jnp.broadcast_to(row[:, i : i + 128], (128, 128)).T for i in range(0, n, 128)
    ]
    return parts[0] if len(parts) == 1 else jnp.concatenate(parts, axis=0)


def lane_sums(x):
    n = x.shape[0]
    parts = [
        jnp.sum(x[i : i + 128].T, axis=0, keepdims=True) for i in range(0, n, 128)
    ]
    return parts[0] if len(parts) == 1 else jnp.concatenate(parts, axis=1)


def state_kernel(core, k_own, v_own, s_own, got, docs, t_out, k_out):
    c = core[0]
    tb, width = k_own.shape
    chip_docs = docs[...]
    last = chip_docs[:, 2 * tb - 1 : 2 * tb]
    own_row = jnp.where(c == 0, chip_docs[:, :tb], chip_docs[:, tb:])
    got_row = jnp.where(c == 0, chip_docs[:, tb:], chip_docs[:, :tb])
    own_keep = column(own_row) == last
    got_keep = column(got_row) == last
    zero = jnp.zeros((tb, DH), BF16)
    for h in range(width // DH):
        cols = slice(h * DH, (h + 1) * DH)
        own = jnp.where(own_keep, k_own[:, cols], zero)
        other = jnp.where(got_keep, got[:tb, cols], zero)
        state = dot(own, v_own[:, cols], ((0,), (0,)))
        state += dot(other, got[tb : 2 * tb, cols], ((0,), (0,)))
        t_out[h * DH : (h + 1) * DH, :] = state.astype(BF16)
    t_out[width:, :] = jnp.broadcast_to(last, (PAD, DH)).astype(BF16)
    k_out[pl.ds(pl.multiple_of(c * tb, tb), tb), :] = s_own[...]
    k_out[pl.ds(pl.multiple_of((1 - c) * tb, tb), tb), :] = got[2 * tb :, :]
    tail = jnp.concatenate(
        [
            jnp.broadcast_to(chip_docs[:, i * tb : (i + 1) * tb], (PAD // 2, tb))
            for i in range(2)
        ],
        axis=0,
    )
    k_out[2 * tb :, :] = jnp.zeros((PAD, width), BF16)
    k_out[2 * tb :, :tb] = tail.astype(BF16)


def intra_kernel(
    core, q_own, k_own, v_own, g_own, got_kv, got_qg, gain, docs,
    intra, q_out, gate_out, k_all, v_all, g_all,
):
    c = core[0]
    tb, width = q_own.shape
    mine = pl.ds(pl.multiple_of(c * tb, tb), tb)
    theirs = pl.ds(pl.multiple_of((1 - c) * tb, tb), tb)
    for whole, own, other in (
        (q_out, q_own, got_qg[:tb]),
        (g_all, g_own, got_qg[tb : 2 * tb]),
        (k_all, k_own, got_kv[:tb]),
        (v_all, v_own, got_kv[tb : 2 * tb]),
    ):
        whole[mine, :] = own[...]
        whole[theirs, :] = other
    n = 2 * tb
    row = lax.broadcasted_iota(jnp.int32, (n, n), 0)
    col = lax.broadcasted_iota(jnp.int32, (n, n), 1)
    d = column(docs[...])
    same = jnp.concatenate([d, d], axis=1) == docs[...]
    visible = same & (row >= col)
    for h in range(width // DH):
        cols = slice(h * DH, (h + 1) * DH)
        scores = dot(q_out[:, cols], k_all[:, cols], ((1,), (1,)))
        weights = jnp.where(visible, scores, 0.0).astype(BF16)
        intra[:, cols] = dot(weights, v_all[:, cols])
        gate = jax.nn.sigmoid(g_all[:, cols].astype(F32))
        gate_out[:, cols] = gate * gain[:, cols].astype(F32)


def mixed_kernel(intra, q, t_got, docs, mixed, squares):
    n, width = q.shape
    seen = column(docs[...]) == t_got[width : width + 1, :].astype(F32)
    total = jnp.zeros((n, DH), F32)
    for h in range(width // DH):
        cols = slice(h * DH, (h + 1) * DH)
        carried = dot(q[:, cols], t_got[h * DH : (h + 1) * DH, :])
        value = intra[:, cols] + jnp.where(seen, carried, 0.0)
        mixed[:, cols] = value
        total += value * value
    squares[...] = lane_sums(total)


def second_kernel(mixed, q, t_got, t_far, docs, fixed, squares):
    n, width = mixed.shape
    near = t_got[width : width + 1, :].astype(F32)
    far = t_far[width : width + 1, :].astype(F32)
    seen = (column(docs[:, :n]) == near) & (near == far)
    total = jnp.zeros((n, DH), F32)
    for h in range(width // DH):
        cols = slice(h * DH, (h + 1) * DH)
        carried = dot(q[:, cols], t_far[h * DH : (h + 1) * DH, :])
        value = mixed[:, cols] + jnp.where(seen, carried, 0.0)
        fixed[:, cols] = value
        total += value * value
    squares[...] = lane_sums(total)


def norm_kernel(columns, mixed, gate, s0, s1, s2, s3, out):
    width = mixed.shape[1]
    total = s0[...] + s1[...] + s2[...] + s3[...]
    scale = column(lax.rsqrt(total / columns + 1e-05))
    for h in range(width // DH):
        cols = slice(h * DH, (h + 1) * DH)
        out[:, cols] = (mixed[:, cols] * scale * gate[:, cols]).astype(BF16)


def output_kernel(columns, core, fixed, gate, s0, s1, s2, s3, rest, out, kept, sent):
    c = core[0]
    tb = fixed.shape[0]
    norm_kernel(columns, fixed, gate, s0, s1, s2, s3, out.at[:tb])
    out[tb:, :] = rest[tb:, :]
    kept[...] = out[pl.ds(pl.multiple_of(c * tb, tb), tb), :]
    sent[...] = out[pl.ds(pl.multiple_of((1 - c) * tb, tb), tb), :]


def weights_kernel(core, q_own, got_q, k_chip, k_near, k_far, docs, weights, q_all, k_all):
    c = core[0]
    tb, width = q_own.shape
    n = 2 * tb
    q_all[pl.ds(pl.multiple_of(c * tb, tb), tb), :] = q_own[...]
    q_all[pl.ds(pl.multiple_of((1 - c) * tb, tb), tb), :] = got_q[2 * tb :, :]
    k_all[:tb, :] = k_far[:tb, :]
    k_all[tb : 3 * tb, :] = k_near[:n, :]
    k_all[3 * tb :, :] = k_chip[:n, :]
    keys = 5 * tb
    half = PAD // 2
    key_docs = jnp.concatenate(
        [
            k_far[tb + half : tb + half + 1, :tb].astype(F32),
            k_near[n : n + 1, :tb].astype(F32),
            k_near[n + half : n + half + 1, :tb].astype(F32),
            docs[...],
        ],
        axis=1,
    )
    d = column(docs[...])
    same = jnp.concatenate([d] * (keys // 128), axis=1) == key_docs
    row = lax.broadcasted_iota(jnp.int32, (n, keys), 0)
    col = lax.broadcasted_iota(jnp.int32, (n, keys), 1) - 3 * tb
    visible = same & (row >= col)
    scale = 1.0 / math.sqrt(DH)
    for h in range(width // DH):
        cols = slice(h * DH, (h + 1) * DH)
        scores = dot(q_all[:, cols], k_all[:, cols], ((1,), (1,))) * scale
        scores = jnp.where(visible, scores, -1e30)
        top = jnp.max(scores, axis=1, keepdims=True)
        e = jnp.exp(scores - top)
        weights[h] = (e / jnp.sum(e, axis=1, keepdims=True)).astype(BF16)


def attend_kernel(core, weights, v_far, v_near, v_own, kept, sent, out):
    c = core[0]
    n, width = v_own.shape
    tb = n // 2
    for h in range(width // DH):
        cols = slice(h * DH, (h + 1) * DH)
        total = dot(weights[h, :, :tb], v_far[:, cols])
        total += dot(weights[h, :, tb : 3 * tb], v_near[:, cols])
        total += dot(weights[h, :, 3 * tb :], v_own[:, cols])
        out[:, cols] = total.astype(BF16)
    kept[...] = out[pl.ds(pl.multiple_of(c * tb, tb), tb), :]
    sent[...] = out[pl.ds(pl.multiple_of((1 - c) * tb, tb), tb), :]


def join_kernel(core, kept, got, out):
    c = core[0]
    width = kept.shape[1]
    out[:, pl.ds(pl.multiple_of(c * width, DH), width)] = kept[...]
    out[:, pl.ds(pl.multiple_of((1 - c) * width, DH), width)] = got[...]


def run(kernel, core, ins, outs, scratch=(), cost=(0, 0)):
    def spec(shape):
        return pl.BlockSpec(shape, lambda i, c, r=len(shape): (0,) * r)

    in_specs, operands = [], []
    for x in ins:
        if isinstance(x, tuple):
            x = x[0]
            shape = (x.shape[0], x.shape[1] // 2)
            in_specs.append(pl.BlockSpec(shape, lambda i, c: (0, c[0])))
        else:
            in_specs.append(spec(x.shape))
        operands.append(x)
    if core is None:
        plain = kernel

        def kernel(_, *refs):
            plain(*refs)

        core = jnp.zeros((1,), jnp.int32)
    out_shape = [jax.ShapeDtypeStruct(s, t) for s, t in outs]
    got = pl.pallas_call(
        kernel,
        out_shape=out_shape,
        grid_spec=pltpu.PrefetchScalarGridSpec(
            num_scalar_prefetch=1,
            grid=(1,),
            in_specs=in_specs,
            out_specs=[spec(s) for s, _ in outs],
            scratch_shapes=[pltpu.VMEM(s, t) for s, t in scratch],
        ),
        compiler_params=pltpu.CompilerParams(vmem_limit_bytes=VMEM_LIMIT),
        cost_estimate=pl.CostEstimate(flops=cost[0], bytes_accessed=cost[1], transcendentals=0),
    )(core, *operands)
    return got[0] if len(got) == 1 else got


def swap(x):
    return lax.ppermute(x, "inner", [(0, 1), (1, 0)])


def next_chip(x):
    chips = lax.axis_size("outer")
    return lax.ppermute(x, "outer", [(i, i + 1) for i in range(chips - 1)])


def over_heads(x):
    size = lax.axis_size("heads")
    x = x + swap(x)
    if size == 4:
        others = [lax.ppermute(x, "heads", [(i, i ^ k) for i in range(size)]) for k in (1, 2, 3)]
        return [x, *others]
    total = lax.psum(x, "heads")
    zero = jnp.zeros_like(total)
    return [total, zero, zero, zero]


def per_device(
    lin_query, lin_key, lin_value, gate_input, norm_gain, segment_ids, soft_query, soft_key
):
    tb, local = lin_query.shape
    width = local // 2
    n = 2 * tb
    heads = width // DH
    columns = local * lax.axis_size("heads")
    c = lax.axis_index("inner")
    core = c.astype(jnp.int32)[None]

    def theirs(*arrays):
        return jnp.concatenate(
            [lax.dynamic_slice_in_dim(a, (1 - c) * width, width, 1) for a in arrays], axis=0
        )

    own_docs = (segment_ids + 1).astype(jnp.int32)[None]
    got_docs = swap(own_docs)
    got_kv = swap(theirs(lin_key, lin_value, soft_key))
    got_qg = swap(theirs(lin_query, gate_input, soft_query))
    docs = jnp.where(
        c == 0,
        jnp.concatenate([own_docs, got_docs], axis=1),
        jnp.concatenate([got_docs, own_docs], axis=1),
    ).astype(F32)

    t_msg, k_msg = run(
        state_kernel,
        core,
        [(lin_key, 0), (lin_value, 0), (soft_key, 0), got_kv, docs],
        [((width + PAD, DH), BF16), ((n + PAD, width), BF16)],
    )
    t_near = next_chip(t_msg)
    k_near = next_chip(k_msg)
    intra, queries, gate = run(
        intra_kernel,
        core,
        [
            (lin_query, 0), (lin_key, 0), (lin_value, 0), (gate_input, 0), got_kv, got_qg,
            (norm_gain[None], 0), docs,
        ],
        [((n, width), F32), ((n, width), BF16), ((n, width), F32)],
        [((n, width), BF16)] * 3,
    )
    mixed, squares = run(
        mixed_kernel, None, [intra, queries, t_near, docs], [((n, width), F32), ((1, n), F32)]
    )
    t_far = next_chip(t_near)
    k_far = next_chip(k_near[tb:])
    values = run(
        functools.partial(norm_kernel, columns),
        None,
        [mixed, gate, *over_heads(squares)],
        [((n, width), BF16)],
    )
    v_near = next_chip(values)
    fixed, squares = run(
        second_kernel,
        None,
        [mixed[:tb], queries[:tb], t_near, t_far, docs],
        [((tb, width), F32), ((1, tb), F32)],
    )
    own, kept, sent = run(
        functools.partial(output_kernel, columns),
        core,
        [fixed, gate[:tb], *over_heads(squares), values],
        [((n, width), BF16), ((tb, width), BF16), ((tb, width), BF16)],
    )
    linear_out = run(join_kernel, core, [kept, swap(sent)], [((tb, local), BF16)])
    weights = run(
        weights_kernel,
        core,
        [(soft_query, 0), got_qg, k_msg, k_near, k_far, docs],
        [((heads, n, 5 * tb), BF16)],
        [((n, width), BF16), ((5 * tb, width), BF16)],
    )
    v_far = next_chip(v_near[tb:])
    kept, sent = run(
        attend_kernel,
        core,
        [weights, v_far, v_near, own],
        [((tb, width), BF16), ((tb, width), BF16)],
        [((n, width), BF16)],
    )
    attended = run(join_kernel, core, [kept, swap(sent)], [((tb, local), BF16)])
    return linear_out, attended


def solution(mesh):
    tokens = P(("outer", "inner"), "heads")
    return jax.shard_map(
        per_device,
        mesh=mesh,
        in_specs=(tokens, tokens, tokens, tokens, P("heads"), P(("outer", "inner")), tokens, tokens),
        out_specs=(tokens, tokens),
        check_vma=False,
    )
```

```python
import functools
import math

import jax
import jax.numpy as jnp
from jax import lax
from jax.experimental import pallas as pl
from jax.experimental.pallas import tpu as pltpu
from jax.sharding import PartitionSpec as P

DH = 128
PAD = 16
F32 = jnp.float32
BF16 = jnp.bfloat16
NONE = -1e30
VMEM_LIMIT = 20 * 1024 * 1024
BYTES_PER_US = 3.0e6


def dot(a, b, dims=((1,), (0,))):
    return lax.dot_general(a, b, (dims, ((), ())), preferred_element_type=F32)


def column(row):
    n = row.shape[1]
    parts = [jnp.broadcast_to(row[:, i : i + 128], (128, 128)).T for i in range(0, n, 128)]
    return parts[0] if len(parts) == 1 else jnp.concatenate(parts, axis=0)


def as_row(col):
    return jnp.broadcast_to(col, (128, 128)).T[:1]


def lane_sums(x):
    parts = [
        jnp.sum(x[i : i + 128].T, axis=0, keepdims=True) for i in range(0, x.shape[0], 128)
    ]
    return parts[0] if len(parts) == 1 else jnp.concatenate(parts, axis=1)


def split(x):
    high = x.astype(BF16)
    rest = x - high.astype(F32)
    middle = rest.astype(BF16)
    return high, middle, (rest - middle.astype(F32)).astype(BF16)


def inner():
    return lax.axis_index("inner")


def chip():
    return lax.axis_index("outer")


def in_order(own, other):
    first = inner() == 0
    return jnp.where(first, own, other), jnp.where(first, other, own)


def mine(width, h=0, heads=None):
    size = width if heads is None else DH
    return pl.ds(pl.multiple_of(inner() * width + h * DH, DH), size)


def head(width, h):
    return mine(width, h, 1)


def place(whole, own, other):
    tb, width = own.shape[0], whole.shape[1]
    cols = mine(width)
    whole[:tb, :], whole[tb:, :] = in_order(own[:, cols], other[:, cols])


def message_docs(message, valid):
    tail = jnp.where(valid, message[message.shape[0] - PAD :, :DH].astype(F32), 0.0)
    half = PAD // 2
    return tail[:1], tail[half : half + 1], tail[PAD - 1 :, DH - 1 :]


def cut_kernel(key, value, segments, keys, values, docs):
    cols = mine(keys.shape[1])
    keys[...] = key[:, cols]
    values[...] = value[:, cols]
    docs[...] = (segments[...] + 1).astype(F32)


def state_kernel(k_own, v_own, k_got, v_got, own_docs, got_docs, t_out, docs):
    tb, width = k_own.shape
    own_row = own_docs[...]
    got_row = (got_docs[...] + 1).astype(F32)
    rows = in_order(own_row, got_row)
    last = rows[1][:, tb - 1 :]
    own_keep = column(own_row) == last
    got_keep = column(got_row) == last
    zero = jnp.zeros((tb, DH), BF16)
    for h in range(width // DH):
        cols, got = slice(h * DH, (h + 1) * DH), head(width, h)
        own = jnp.where(own_keep, k_own[:, cols], zero)
        other = jnp.where(got_keep, k_got[:, got], zero)
        state = dot(own, v_own[:, cols], ((0,), (0,)))
        state += dot(other, v_got[:, got], ((0,), (0,)))
        t_out[:DH, cols] = state.astype(BF16)
    half = PAD // 2
    tail = jnp.concatenate([jnp.broadcast_to(r, (half, tb)) for r in rows], axis=0)
    t_out[DH:, :] = jnp.zeros((PAD, width), BF16)
    t_out[DH:, :tb] = tail.astype(BF16)
    docs[...] = jnp.concatenate(rows, axis=1)


def intra_kernel(
    q_own, k_own, v_own, g_own, q_got, k_got, v_got, g_got, gain, docs,
    intra, q_out, gate_out, k_all, v_all, g_all,
):
    n, width = intra.shape
    tb = n // 2
    place(q_out, q_own, q_got)
    place(g_all, g_own, g_got)
    cols = mine(width)
    k_all[:tb, :], k_all[tb:, :] = in_order(k_own[...], k_got[:, cols])
    v_all[:tb, :], v_all[tb:, :] = in_order(v_own[...], v_got[:, cols])
    row = lax.broadcasted_iota(jnp.int32, (n, n), 0)
    col = lax.broadcasted_iota(jnp.int32, (n, n), 1)
    d = column(docs[...])
    same = jnp.concatenate([d, d], axis=1) == docs[...]
    visible = same & (row >= col)
    gains = gain[:, mine(width)].astype(F32)
    for h in range(width // DH):
        cols = slice(h * DH, (h + 1) * DH)
        scores = dot(q_out[:, cols], k_all[:, cols], ((1,), (1,)))
        weights = jnp.where(visible, scores, 0.0).astype(BF16)
        intra[:, cols] = dot(weights, v_all[:, cols])
        gate = jax.nn.sigmoid(g_all[:, cols].astype(F32))
        gate_out[:, cols] = gate * gains[:, cols]


def mixed_kernel(intra, q, t_near, docs, mixed, squares):
    n, width = q.shape
    seen = column(docs[...]) == message_docs(t_near, chip() >= 1)[2]
    total = jnp.zeros((n, DH), F32)
    for h in range(width // DH):
        cols = slice(h * DH, (h + 1) * DH)
        carried = dot(q[:, cols], t_near[:DH, cols])
        value = intra[:, cols] + jnp.where(seen, carried, 0.0)
        mixed[:, cols] = value
        total += value * value
    squares[...] = lane_sums(total)


def second_kernel(mixed, q, t_near, message, docs, fixed, squares):
    n, width = fixed.shape
    near = message_docs(t_near, chip() >= 1)[2]
    far = message_docs(message, chip() >= 2)[2]
    seen = (column(docs[:, :n]) == near) & (near == far)
    total = jnp.zeros((n, DH), F32)
    for h in range(width // DH):
        cols = slice(h * DH, (h + 1) * DH)
        carried = dot(q[:n, cols], message[2 * n : 2 * n + DH, cols])
        value = mixed[:n, cols] + jnp.where(seen, carried, 0.0)
        fixed[:, cols] = value
        total += value * value
    squares[...] = lane_sums(total)


def normed(columns, mixed, gate, sums, out):
    scale = column(lax.rsqrt(sum(x[...] for x in sums) / columns + 1e-05))
    for h in range(mixed.shape[1] // DH):
        cols = slice(h * DH, (h + 1) * DH)
        out[:, cols] = (mixed[:, cols] * scale * gate[:, cols]).astype(BF16)


def norm_kernel(columns, mixed, gate, s0, s1, s2, s3, t_near, out):
    n = mixed.shape[0]
    normed(columns, mixed, gate, (s0, s1, s2, s3), out.at[pl.ds(0, n)])
    out[n:, :] = t_near[...]


def output_kernel(columns, fixed, gate, s0, s1, s2, s3, values, first, out, sent):
    tb = fixed.shape[0]
    normed(columns, fixed, gate.at[pl.ds(0, tb)], (s0, s1, s2, s3), first)
    top = inner() == 0
    out[...] = jnp.where(top, first[...], values[tb : 2 * tb, :])
    sent[...] = jnp.where(top, values[tb : 2 * tb, :], first[...])


def softmax_part(q, k, visible):
    scores = dot(q, k, ((1,), (1,))) * (1.0 / math.sqrt(DH))
    scores = jnp.where(visible, scores, NONE)
    top = jnp.max(scores, axis=1, keepdims=True)
    e = jnp.where(visible, jnp.exp(scores - top), 0.0)
    total = jnp.sum(e, axis=1, keepdims=True)
    some = jnp.where(total > 0.0, total, 1.0)
    return (e / some).astype(BF16), jnp.where(total > 0.0, top + jnp.log(some), NONE)


def pick_kernel(first, second, out):
    out[...] = jnp.where(inner() == 0, first[...], second[...])


def far_kernel(mixed_own, mixed_got, k_own, k_got, t_near, docs, weights, lse):
    tb, local = k_own.shape
    width = local // 2
    near = message_docs(t_near, chip() >= 1)
    last = docs[:, 2 * tb - 1 :]
    visible = jnp.broadcast_to((near[1] == last) & (near[2] == last), (tb, tb))
    for h in range(width // DH):
        cols = head(width, h)
        queries = in_order(mixed_own[:, cols], mixed_got[:, cols])[1]
        keys = in_order(k_own[:, cols], k_got[:, cols])[0]
        weights[h], top = softmax_part(queries, keys, visible)
        lse[:, h * DH : (h + 1) * DH] = as_row(top)


def answer_kernel(weights, lse, values, out):
    tb = weights.shape[1]
    width = values.shape[1]
    for h in range(width // DH):
        cols = slice(h * DH, (h + 1) * DH)
        out[:tb, cols] = dot(weights[h], values[tb : 2 * tb, cols]).astype(BF16)
    high, middle, low = split(lse[...])
    rows = [high, middle, low, jnp.zeros((PAD - 3, width), BF16)]
    out[tb:, :] = jnp.concatenate([r.astype(F32) for r in rows], axis=0).astype(BF16)


def weights_kernel(
    q_own, k_own, q_got, k_got, near_first, near_first_got, near_last, near_last_got,
    t_near, docs, weights, lse, q_all, k_all,
):
    n, width = q_all.shape
    tb = n // 2
    keys = 2 * n
    place(q_all, q_own, q_got)
    cols = mine(width)
    k_all[:tb, :] = in_order(near_first[:, cols], near_first_got[:, cols])[0]
    k_all[tb:n, :] = in_order(near_last[:, cols], near_last_got[:, cols])[0]
    place(k_all.at[n:], k_own, k_got)
    near_docs = message_docs(t_near, chip() >= 1)
    key_docs = jnp.concatenate([near_docs[0], near_docs[1], docs[...]], axis=1)
    d = column(docs[...])
    same = jnp.concatenate([d] * (keys // 128), axis=1) == key_docs
    row = lax.broadcasted_iota(jnp.int32, (n, keys), 0)
    col = lax.broadcasted_iota(jnp.int32, (n, keys), 1) - n
    visible = same & (row >= col)
    for h in range(width // DH):
        cols = slice(h * DH, (h + 1) * DH)
        weights[h], top = softmax_part(q_all[:, cols], k_all[:, cols], visible)
        lse[:, cols] = as_row(top[:tb])


def attend_kernel(weights, lse, answer, near, first, values, t_near, docs, out, sent):
    tb, width = first.shape
    n = 2 * tb
    near_last = message_docs(t_near, chip() >= 2)[2]
    asked = column(docs[:, :tb]) == near_last
    for h in range(width // DH):
        cols = slice(h * DH, (h + 1) * DH)
        total = dot(weights[h, :, :n], near[:n, cols])
        total += dot(weights[h, :, n : n + tb], first[:, cols])
        total += dot(weights[h, :, n + tb :], values[tb:n, cols])
        far_lse = sum(answer[tb + i : tb + i + 1, cols].astype(F32) for i in range(3))
        far_lse = jnp.where(asked, column(far_lse), NONE)
        here_lse = column(lse[:, cols])
        top = jnp.maximum(far_lse, here_lse)
        far, here = jnp.exp(far_lse - top), jnp.exp(here_lse - top)
        part = jnp.where(asked, far * answer[:tb, cols].astype(F32), 0.0)
        upper = ((here * total[:tb] + part) / (here + far)).astype(BF16)
        lower = total[tb:].astype(BF16)
        is_first = inner() == 0
        out[:, cols] = jnp.where(is_first, upper, lower)
        sent[:, cols] = jnp.where(is_first, lower, upper)


def join_kernel(kept, got, out):
    width = kept.shape[1]
    out[:, pl.ds(pl.multiple_of(inner() * width, DH), width)] = kept[...]
    out[:, pl.ds(pl.multiple_of((1 - inner()) * width, DH), width)] = got[...]


def run(kernel, ins, outs, scratch=(), us=0.5):
    got = pl.pallas_call(
        kernel,
        out_shape=[jax.ShapeDtypeStruct(*o) for o in outs],
        in_specs=[pl.BlockSpec(memory_space=pltpu.VMEM)] * len(ins),
        out_specs=[pl.BlockSpec(memory_space=pltpu.VMEM)] * len(outs),
        scratch_shapes=scratch,
        compiler_params=pltpu.CompilerParams(vmem_limit_bytes=VMEM_LIMIT),
        cost_estimate=pl.CostEstimate(
            flops=0, bytes_accessed=int(us * BYTES_PER_US), transcendentals=0
        ),
    )(*ins)
    return got[0] if len(got) == 1 else got


def swap(x):
    return lax.ppermute(x, "inner", [(0, 1), (1, 0)])


def next_chip(x):
    chips = lax.axis_size("outer")
    return lax.ppermute(x, "outer", [(i, (i + 1) % chips) for i in range(chips)])


def both_ways(x):
    last = lax.axis_size("outer") - 1
    up = [(2 * i, 2 * i + 2) for i in range(last)] + [(2 * last, 2 * last + 1)]
    down = [(2 * i + 1, 2 * i - 1) for i in range(1, last + 1)] + [(1, 0)]
    return lax.ppermute(x, ("outer", "inner"), up + down)


def over_heads(x):
    size = lax.axis_size("heads")
    x = x + swap(x)
    if size == 4:
        others = [lax.ppermute(x, "heads", [(i, i ^ k) for i in range(size)]) for k in (1, 2, 3)]
        return [x, *others]
    total = lax.psum(x, "heads")
    zero = jnp.zeros_like(total)
    return [total, zero, zero, zero]


def per_device(
    lin_query, lin_key, lin_value, gate_input, norm_gain, segment_ids, soft_query, soft_key
):
    tb, local = lin_query.shape
    width = local // 2
    n = 2 * tb
    heads = width // DH
    columns = local * lax.axis_size("heads")
    block, whole = ((tb, width), BF16), ((n, width), BF16)
    scratch = pltpu.VMEM((n, width), BF16)
    tie = lax.optimization_barrier

    def joined(kept, sent):
        return run(join_kernel, [kept, swap(sent)], [((tb, local), BF16)])

    own_docs = segment_ids[None]
    got_docs = swap(own_docs)
    lk_got, lv_got = swap(lin_key), swap(lin_value)
    keys, values, own_docs = run(
        cut_kernel,
        [lin_key, lin_value, own_docs],
        [block, block, ((1, tb), F32)],
        us=2.0,
    )
    t_msg, docs = run(
        state_kernel,
        [keys, values, lk_got, lv_got, own_docs, got_docs],
        [((DH + PAD, width), BF16), ((1, n), F32)],
    )
    t_near = next_chip(t_msg)
    lin_query, gate_input, soft_query, soft_key, _ = tie(
        (lin_query, gate_input, soft_query, soft_key, t_msg)
    )
    lq_got, g_got = swap(lin_query), swap(gate_input)
    sq_got, sk_got = swap(soft_query), swap(soft_key)
    out_first = run(pick_kernel, [soft_key, sq_got], [((tb, local), BF16)], us=0.3)
    intra, queries, gate = run(
        intra_kernel,
        [
            lin_query, keys, values, gate_input, lq_got, lk_got, lv_got, g_got,
            norm_gain[None], docs,
        ],
        [((n, width), F32), whole, ((n, width), F32)],
        [scratch] * 3,
        us=1.2,
    )
    t_near, intra, out_first, out_last = tie((t_near, intra, out_first, sk_got))
    first_own, last_own = both_ways(out_first), both_ways(out_last)
    first_got, last_got = swap(first_own), swap(last_own)
    mixed, squares = run(
        mixed_kernel, [intra, queries, t_near, docs], [((n, width), F32), ((1, n), F32)]
    )
    values = run(
        functools.partial(norm_kernel, columns),
        [mixed, gate, *over_heads(squares), t_near],
        [((n + DH + PAD, width), BF16)],
        us=0.3,
    )
    near_values = next_chip(values)
    far_weights, far_lse = run(
        far_kernel,
        [first_own, first_got, last_own, last_got, t_near, docs],
        [((heads, tb, tb), BF16), ((1, width), F32)],
    )
    weights, lse = run(
        weights_kernel,
        [
            soft_query, soft_key, sq_got, sk_got, first_own, first_got, last_own, last_got,
            t_near, docs,
        ],
        [((heads, n, 2 * n), BF16), ((1, width), F32)],
        [scratch, pltpu.VMEM((2 * n, width), BF16)],
        us=2.5,
    )
    far_weights, weights, near_values = tie((far_weights, weights, near_values))
    answer = next_chip(
        run(
            answer_kernel, [far_weights, far_lse, near_values], [((tb + PAD, width), BF16)], us=0.3
        )
    )
    fixed, squares = run(
        second_kernel,
        [mixed, queries, t_near, near_values, docs],
        [((tb, width), F32), ((1, tb), F32)],
    )
    first, kept, sent = run(
        functools.partial(output_kernel, columns),
        [fixed, gate, *over_heads(squares), values],
        [block] * 3,
        us=0.3,
    )
    linear_out = joined(kept, sent)
    kept, sent = run(
        attend_kernel,
        [weights, lse, answer, near_values, first, values, t_near, docs],
        [block, block],
        us=1.0,
    )
    return linear_out, joined(kept, sent)


def solution(mesh):
    tokens = P(("outer", "inner"), "heads")
    return jax.shard_map(
        per_device,
        mesh=mesh,
        in_specs=(tokens, tokens, tokens, tokens, P("heads"), P(("outer", "inner")), tokens, tokens),
        out_specs=(tokens, tokens),
        check_vma=False,
    )
```

```python
import functools
import math

import jax
import jax.numpy as jnp
from jax import lax
from jax.experimental import pallas as pl
from jax.experimental.pallas import tpu as pltpu
from jax.sharding import PartitionSpec as P

DH = 128
PAD = 16
F32 = jnp.float32
BF16 = jnp.bfloat16
NONE = -1e30
VMEM_LIMIT = 20 * 1024 * 1024
BYTES_PER_US = 3.0e6


def dot(a, b, dims=((1,), (0,))):
    return lax.dot_general(a, b, (dims, ((), ())), preferred_element_type=F32)


def column(row):
    n = row.shape[1]
    parts = [jnp.broadcast_to(row[:, i : i + 128], (128, 128)).T for i in range(0, n, 128)]
    return parts[0] if len(parts) == 1 else jnp.concatenate(parts, axis=0)


def as_row(col):
    return jnp.broadcast_to(col, (128, 128)).T[:1]


def lane_sums(x):
    parts = [
        jnp.sum(x[i : i + 128].T, axis=0, keepdims=True) for i in range(0, x.shape[0], 128)
    ]
    return parts[0] if len(parts) == 1 else jnp.concatenate(parts, axis=1)


def split(x):
    high = x.astype(BF16)
    rest = x - high.astype(F32)
    middle = rest.astype(BF16)
    return high, middle, (rest - middle.astype(F32)).astype(BF16)


def inner():
    return lax.axis_index("inner")


def chip():
    return lax.axis_index("outer")


def in_order(own, other):
    first = inner() == 0
    return jnp.where(first, own, other), jnp.where(first, other, own)


def mine(width, h=0, heads=None):
    size = width if heads is None else DH
    return pl.ds(pl.multiple_of(inner() * width + h * DH, DH), size)


def head(width, h):
    return mine(width, h, 1)


def place(whole, own, other):
    tb, width = own.shape[0], whole.shape[1]
    cols = mine(width)
    whole[:tb, :], whole[tb:, :] = in_order(own[:, cols], other[:, cols])


def message_docs(message, valid):
    tail = jnp.where(valid, message[message.shape[0] - PAD :, :DH].astype(F32), 0.0)
    half = PAD // 2
    return tail[:1], tail[half : half + 1], tail[PAD - 1 :, DH - 1 :]


def cut_kernel(key, value, segments, keys, values, docs):
    cols = mine(keys.shape[1])
    keys[...] = key[:, cols]
    values[...] = value[:, cols]
    docs[...] = (segments[...] + 1).astype(F32)


def state_kernel(k_own, v_own, k_got, v_got, own_docs, got_docs, t_out, docs):
    tb, width = k_own.shape
    own_row = own_docs[...]
    got_row = (got_docs[...] + 1).astype(F32)
    rows = in_order(own_row, got_row)
    last = rows[1][:, tb - 1 :]
    own_keep = column(own_row) == last
    got_keep = column(got_row) == last
    zero = jnp.zeros((tb, DH), BF16)
    for h in range(width // DH):
        cols, got = slice(h * DH, (h + 1) * DH), head(width, h)
        own = jnp.where(own_keep, k_own[:, cols], zero)
        other = jnp.where(got_keep, k_got[:, got], zero)
        state = dot(own, v_own[:, cols], ((0,), (0,)))
        state += dot(other, v_got[:, got], ((0,), (0,)))
        t_out[:DH, cols] = state.astype(BF16)
    half = PAD // 2
    tail = jnp.concatenate([jnp.broadcast_to(r, (half, tb)) for r in rows], axis=0)
    t_out[DH:, :] = jnp.zeros((PAD, width), BF16)
    t_out[DH:, :tb] = tail.astype(BF16)
    docs[...] = jnp.concatenate(rows, axis=1)


def intra_kernel(
    q_own, k_own, v_own, g_own, q_got, k_got, v_got, g_got, gain, docs,
    intra, q_out, gate_out, squares, k_all, v_all, g_all,
):
    n, width = intra.shape
    tb = n // 2
    place(q_out, q_own, q_got)
    place(g_all, g_own, g_got)
    cols = mine(width)
    k_all[:tb, :], k_all[tb:, :] = in_order(k_own[...], k_got[:, cols])
    v_all[:tb, :], v_all[tb:, :] = in_order(v_own[...], v_got[:, cols])
    row = lax.broadcasted_iota(jnp.int32, (n, n), 0)
    col = lax.broadcasted_iota(jnp.int32, (n, n), 1)
    d = column(docs[...])
    same = jnp.concatenate([d, d], axis=1) == docs[...]
    visible = same & (row >= col)
    gains = gain[:, mine(width)].astype(F32)
    total = jnp.zeros((n, DH), F32)
    for h in range(width // DH):
        cols = slice(h * DH, (h + 1) * DH)
        scores = dot(q_out[:, cols], k_all[:, cols], ((1,), (1,)))
        weights = jnp.where(visible, scores, 0.0).astype(BF16)
        value = dot(weights, v_all[:, cols])
        intra[:, cols] = value
        total += value * value
        gate = jax.nn.sigmoid(g_all[:, cols].astype(F32))
        gate_out[:, cols] = gate * gains[:, cols]
    squares[...] = lane_sums(total)


def mixed_kernel(intra, q, t_near, t_far, docs, mixed, squares):
    n, width = q.shape
    tb = n // 2
    seen = column(docs[...]) == message_docs(t_near, chip() >= 1)[2]
    both = spanning(t_near, t_far, docs)
    total = jnp.zeros((n, DH), F32)
    for h in range(width // DH):
        cols = slice(h * DH, (h + 1) * DH)
        value = intra[:, cols] + jnp.where(seen, dot(q[:, cols], t_near[:DH, cols]), 0.0)
        first = jnp.where(both, dot(q[:tb, cols], t_far[:DH, cols]), 0.0)
        value = jnp.concatenate([value[:tb] + first, value[tb:]], axis=0)
        mixed[:, cols] = value
        total += value * value
    squares[...] = lane_sums(total)


def spanning(t_near, t_far, docs):
    near = message_docs(t_near, chip() >= 1)[2]
    far = message_docs(t_far, chip() >= 2)[2]
    return (column(docs[:, : docs.shape[1] // 2]) == near) & (near == far)


def normed(columns, mixed, gate, sums, out):
    scale = column(lax.rsqrt(sum(x[...] for x in sums) / columns + 1e-05))
    for h in range(mixed.shape[1] // DH):
        cols = slice(h * DH, (h + 1) * DH)
        out[:, cols] = (mixed[:, cols] * scale * gate[:, cols]).astype(BF16)


def norm_kernel(columns, mixed, gate, s0, s1, s2, out):
    normed(columns, mixed, gate, (s0, s1, s2), out)


def output_kernel(columns, mixed, gate, s0, s1, s2, out, kept, sent):
    tb = kept.shape[0]
    normed(columns, mixed, gate, (s0, s1, s2), out)
    kept[...], sent[...] = in_order(out[:tb, :], out[tb:, :])


def softmax_part(q, k, visible):
    scores = dot(q, k, ((1,), (1,))) * (1.0 / math.sqrt(DH))
    scores = jnp.where(visible, scores, NONE)
    top = jnp.max(scores, axis=1, keepdims=True)
    e = jnp.where(visible, jnp.exp(scores - top), 0.0)
    total = jnp.sum(e, axis=1, keepdims=True)
    some = jnp.where(total > 0.0, total, 1.0)
    return (e / some).astype(BF16), jnp.where(total > 0.0, top + jnp.log(some), NONE)


def pick_kernel(first, second, out):
    out[...] = jnp.where(inner() == 0, first[...], second[...])


def far_kernel(own, got, k_own, k_got, t_near, docs, weights, lse, k_all):
    tb, width = k_own.shape[0], k_all.shape[1]
    n = 2 * tb
    cols = mine(width)
    k_all[:tb, :], queries = in_order(own[:, cols], got[:, cols])
    place(k_all.at[tb:], k_own, k_got)
    near = message_docs(t_near, chip() >= 1)
    last = docs[:, n - 1 :]
    key_docs = jnp.concatenate([near[1], docs[...]], axis=1)
    visible = jnp.broadcast_to((key_docs == last) & (near[2] == last), (tb, 3 * tb))
    for h in range(width // DH):
        cols = slice(h * DH, (h + 1) * DH)
        weights[h], top = softmax_part(queries[:, cols], k_all[:, cols], visible)
        lse[:, cols] = as_row(top)


def answer_kernel(weights, lse, near_values, values, out):
    n, width = values.shape
    tb = n // 2
    for h in range(width // DH):
        cols = slice(h * DH, (h + 1) * DH)
        total = dot(weights[h, :, :tb], near_values[tb:, cols])
        total += dot(weights[h, :, tb:], values[:, cols])
        out[:tb, cols] = total.astype(BF16)
    high, middle, low = split(lse[...])
    rows = [high, middle, low, jnp.zeros((PAD - 3, width), BF16)]
    out[tb:, :] = jnp.concatenate([r.astype(F32) for r in rows], axis=0).astype(BF16)


def weights_kernel(
    q_own, k_own, q_got, k_got, near_first, near_first_got, near_last, near_last_got,
    t_near, docs, weights, first_weights, first_lse, q_all, k_all,
):
    n, width = q_all.shape
    tb = n // 2
    keys = 2 * n
    place(q_all, q_own, q_got)
    cols = mine(width)
    k_all[:tb, :] = in_order(near_first[:, cols], near_first_got[:, cols])[0]
    k_all[tb:n, :] = in_order(near_last[:, cols], near_last_got[:, cols])[0]
    place(k_all.at[n:], k_own, k_got)
    near_docs = message_docs(t_near, chip() >= 1)
    key_docs = jnp.concatenate([near_docs[0], near_docs[1], docs[...]], axis=1)
    d = column(docs[...])
    same = jnp.concatenate([d] * (keys // 128), axis=1) == key_docs
    row = lax.broadcasted_iota(jnp.int32, (n, keys), 0)
    col = lax.broadcasted_iota(jnp.int32, (n, keys), 1) - n
    visible = same & (row >= col)
    for h in range(width // DH):
        cols = slice(h * DH, (h + 1) * DH)
        weights[h], _ = softmax_part(q_all[:, cols], k_all[:, cols], visible)
        block = slice(n, n + tb)
        first_weights[h], top = softmax_part(
            q_all[:tb, cols], k_all[block, cols], visible[:tb, block]
        )
        first_lse[:, cols] = as_row(top)


def attend_kernel(weights, near, values, kept, sent):
    n, width = values.shape
    tb = n // 2
    top = inner() == 0
    for h in range(width // DH):
        cols = slice(h * DH, (h + 1) * DH)
        total = dot(weights[h, :, :n], near[:, cols])
        total += dot(weights[h, :, n:], values[:, cols])
        first, last = total[:tb].astype(BF16), total[tb:].astype(BF16)
        kept[:, cols] = jnp.where(top, first, last)
        sent[:, cols] = jnp.where(top, last, first)


def merge_kernel(
    weights, lse, values, answer, t_near, t_far, docs, kept, sent, new_kept, new_sent
):
    tb, width = kept.shape
    asked = spanning(t_near, t_far, docs)
    top_block = inner() == 0
    for h in range(width // DH):
        cols = slice(h * DH, (h + 1) * DH)
        far_lse = sum(answer[tb + i : tb + i + 1, cols].astype(F32) for i in range(3))
        top = jnp.maximum(far_lse, lse[:, cols])
        far, here = jnp.exp(far_lse - top), jnp.exp(lse[:, cols] - top)
        far, here = column(far / (far + here)), column(here / (far + here))
        merged = here * dot(weights[h], values[:tb, cols]) + far * answer[:tb, cols].astype(F32)
        before, other = in_order(kept[:, cols], sent[:, cols])
        rows = jnp.where(asked, merged.astype(BF16), before)
        new_kept[:, cols] = jnp.where(top_block, rows, other)
        new_sent[:, cols] = jnp.where(top_block, other, rows)


def join_kernel(kept, got, out):
    width = kept.shape[1]
    out[:, pl.ds(pl.multiple_of(inner() * width, DH), width)] = kept[...]
    out[:, pl.ds(pl.multiple_of((1 - inner()) * width, DH), width)] = got[...]


def run(kernel, ins, outs, scratch=(), us=0.5):
    got = pl.pallas_call(
        kernel,
        out_shape=[jax.ShapeDtypeStruct(*o) for o in outs],
        in_specs=[pl.BlockSpec(memory_space=pltpu.VMEM)] * len(ins),
        out_specs=[pl.BlockSpec(memory_space=pltpu.VMEM)] * len(outs),
        scratch_shapes=scratch,
        compiler_params=pltpu.CompilerParams(vmem_limit_bytes=VMEM_LIMIT),
        cost_estimate=pl.CostEstimate(
            flops=0, bytes_accessed=int(us * BYTES_PER_US), transcendentals=0
        ),
    )(*ins)
    return got[0] if len(got) == 1 else got


def swap(x):
    return lax.ppermute(x, "inner", [(0, 1), (1, 0)])


def next_chip(x, line=False):
    chips = lax.axis_size("outer")
    if line:
        return lax.ppermute(x, "outer", [(i, i + 1) for i in range(chips - 1)])
    return lax.ppermute(x, "outer", [(i, (i + 1) % chips) for i in range(chips)])


def both_ways(x):
    last = lax.axis_size("outer") - 1
    up = [(2 * i, 2 * i + 2) for i in range(last)] + [(2 * last, 2 * last + 1)]
    down = [(2 * i + 1, 2 * i - 1) for i in range(1, last + 1)] + [(1, 0)]
    return lax.ppermute(x, ("outer", "inner"), up + down)


def other_heads(x):
    size = lax.axis_size("heads")
    if size != 4:
        return [lax.psum(x, "heads") - x, jnp.zeros_like(x)]
    one = lax.ppermute(x, "heads", [(i, i ^ 1) for i in range(size)])
    return [one, lax.ppermute(x + one, "heads", [(i, i ^ 2) for i in range(size)])]


def over_heads(x):
    x = x + swap(x)
    return [x, *other_heads(x)]


def per_device(
    lin_query, lin_key, lin_value, gate_input, norm_gain, segment_ids, soft_query, soft_key
):
    tb, local = lin_query.shape
    width = local // 2
    n = 2 * tb
    heads = width // DH
    columns = local * lax.axis_size("heads")
    block, whole = ((tb, width), BF16), ((n, width), BF16)
    scratch = pltpu.VMEM((n, width), BF16)
    tie = lax.optimization_barrier

    def joined(kept, sent):
        return run(join_kernel, [kept, swap(sent)], [((tb, local), BF16)])

    own_docs = segment_ids[None]
    got_docs = swap(own_docs)
    lk_got, lv_got = swap(lin_key), swap(lin_value)
    keys, values, own_docs = run(
        cut_kernel, [lin_key, lin_value, own_docs], [block, block, ((1, tb), F32)], us=2.0
    )
    t_msg, docs = run(
        state_kernel,
        [keys, values, lk_got, lv_got, own_docs, got_docs],
        [((DH + PAD, width), BF16), ((1, n), F32)],
    )
    t_near = next_chip(t_msg)
    raw_key = soft_key
    lin_query, gate_input, soft_query, soft_key, _ = tie(
        (lin_query, gate_input, soft_query, soft_key, t_msg)
    )
    lq_got, g_got = swap(lin_query), swap(gate_input)
    sq_got, sk_got = swap(soft_query), swap(soft_key)
    intra, queries, gate, squares = run(
        intra_kernel,
        [
            lin_query, keys, values, gate_input, lq_got, lk_got, lv_got, g_got,
            norm_gain[None], docs,
        ],
        [((n, width), F32), whole, ((n, width), F32), ((1, n), F32)],
        [scratch] * 3,
        us=1.2,
    )
    chip_squares = squares + swap(squares)
    sums = [chip_squares, *other_heads(chip_squares)]
    t_far = next_chip(t_near, line=True)
    sums, t_far = tie((sums, t_far))
    early = run(functools.partial(norm_kernel, columns), [intra, gate, *sums], [whole], us=0.3)
    first_own = both_ways(tie((raw_key, t_msg))[0])
    out_last = run(pick_kernel, [sk_got, sq_got], [((tb, local), BF16)], us=0.3)
    last_own = both_ways(tie((out_last, chip_squares))[0])
    near_values = next_chip(early, line=True)
    mixed, squares = run(
        mixed_kernel, [intra, queries, t_near, t_far, docs], [((n, width), F32), ((1, n), F32)]
    )
    values, lin_kept, lin_sent = run(
        functools.partial(output_kernel, columns),
        [mixed, gate, *over_heads(squares)],
        [whole, block, block],
        us=0.3,
    )
    first_got, last_got = swap(first_own), swap(last_own)
    far_weights, far_lse = run(
        far_kernel,
        [last_own, last_got, soft_key, sk_got, t_near, docs],
        [((heads, tb, 3 * tb), BF16), ((1, width), F32)],
        [pltpu.VMEM((3 * tb, width), BF16)],
        us=1.0,
    )
    far_weights, near_values = tie((far_weights, near_values))
    weights, first_weights, first_lse = run(
        weights_kernel,
        [
            soft_query, soft_key, sq_got, sk_got, first_own, first_got, last_own, last_got,
            t_near, docs,
        ],
        [((heads, n, 2 * n), BF16), ((heads, tb, tb), BF16), ((1, width), F32)],
        [scratch, pltpu.VMEM((2 * n, width), BF16)],
        us=2.5,
    )
    values, near_values = tie((values, near_values))
    answer = next_chip(
        run(
            answer_kernel,
            [far_weights, far_lse, near_values, values],
            [((tb + PAD, width), BF16)],
            us=0.3,
        ),
        line=True,
    )
    linear_out = joined(lin_kept, lin_sent)
    kept, sent = run(attend_kernel, [weights, near_values, values], [block, block], us=0.8)
    kept, sent = run(
        merge_kernel,
        [first_weights, first_lse, values, answer, t_near, t_far, docs, kept, sent],
        [block, block],
    )
    return linear_out, joined(kept, sent)


def solution(mesh):
    tokens = P(("outer", "inner"), "heads")
    return jax.shard_map(
        per_device,
        mesh=mesh,
        in_specs=(tokens, tokens, tokens, tokens, P("heads"), P(("outer", "inner")), tokens, tokens),
        out_specs=(tokens, tokens),
        check_vma=False,
    )
```

```python
import functools
import math

import jax
import jax.numpy as jnp
from jax import lax
from jax.experimental import pallas as pl
from jax.experimental.pallas import tpu as pltpu
from jax.sharding import PartitionSpec as P

DH = 128
PAD = 8
F32 = jnp.float32
BF16 = jnp.bfloat16
NONE = -1e30
VMEM_LIMIT = 20 * 1024 * 1024
BYTES_PER_US = 3.0e6


def dot(a, b, dims=((1,), (0,))):
    return lax.dot_general(a, b, (dims, ((), ())), preferred_element_type=F32)


def column(row):
    n = row.shape[1]
    parts = [jnp.broadcast_to(row[:, i : i + 128], (128, 128)).T for i in range(0, n, 128)]
    return parts[0] if len(parts) == 1 else jnp.concatenate(parts, axis=0)


def as_row(col):
    return jnp.broadcast_to(col, (128, 128)).T[:1]


def lane_sums(x):
    parts = [
        jnp.sum(x[i : i + 128].T, axis=0, keepdims=True) for i in range(0, x.shape[0], 128)
    ]
    return parts[0] if len(parts) == 1 else jnp.concatenate(parts, axis=1)


def split(x):
    high = x.astype(BF16)
    rest = x - high.astype(F32)
    middle = rest.astype(BF16)
    return high, middle, (rest - middle.astype(F32)).astype(BF16)


def inner():
    return lax.axis_index("inner")


def chip():
    return lax.axis_index("outer")


def in_order(own, other):
    first = inner() == 0
    return jnp.where(first, own, other), jnp.where(first, other, own)


def mine(width, h=0, heads=None):
    size = width if heads is None else DH
    return pl.ds(pl.multiple_of(inner() * width + h * DH, DH), size)


def head(width, h):
    return mine(width, h, 1)


def place(whole, own, other):
    tb, width = own.shape[0], whole.shape[1]
    cols = mine(width)
    whole[:tb, :], whole[tb:, :] = in_order(own[:, cols], other[:, cols])


def message_docs(message, valid):
    tail = jnp.where(valid, message[message.shape[0] - PAD :, :DH].astype(F32), 0.0)
    half = PAD // 2
    return tail[:1], tail[half : half + 1], tail[PAD - 1 :, DH - 1 :]


def cut_kernel(key, value, segments, keys, values, docs):
    cols = mine(keys.shape[1])
    keys[...] = key[:, cols]
    values[...] = value[:, cols]
    docs[...] = (segments[...] + 1).astype(F32)


def state_kernel(k_own, v_own, k_got, v_got, own_docs, got_docs, t_out, docs):
    tb, width = k_own.shape
    own_row = own_docs[...]
    got_row = (got_docs[...] + 1).astype(F32)
    rows = in_order(own_row, got_row)
    last = rows[1][:, tb - 1 :]
    own_keep = column(own_row) == last
    got_keep = column(got_row) == last
    zero = jnp.zeros((tb, DH), BF16)
    for h in range(width // DH):
        cols, got = slice(h * DH, (h + 1) * DH), head(width, h)
        own = jnp.where(own_keep, k_own[:, cols], zero)
        other = jnp.where(got_keep, k_got[:, got], zero)
        state = dot(own, v_own[:, cols], ((0,), (0,)))
        state += dot(other, v_got[:, got], ((0,), (0,)))
        t_out[:DH, cols] = state.astype(BF16)
    half = PAD // 2
    tail = jnp.concatenate([jnp.broadcast_to(r, (half, tb)) for r in rows], axis=0)
    t_out[DH:, :] = jnp.zeros((PAD, width), BF16)
    t_out[DH:, :tb] = tail.astype(BF16)
    docs[...] = jnp.concatenate(rows, axis=1)


def intra_kernel(
    q_own, k_own, v_own, g_own, q_got, k_got, v_got, g_got, gain, docs,
    intra, q_out, gate_out, squares, k_all, v_all, g_all,
):
    n, width = intra.shape
    tb = n // 2
    place(q_out, q_own, q_got)
    place(g_all, g_own, g_got)
    cols = mine(width)
    k_all[:tb, :], k_all[tb:, :] = in_order(k_own[...], k_got[:, cols])
    v_all[:tb, :], v_all[tb:, :] = in_order(v_own[...], v_got[:, cols])
    row = lax.broadcasted_iota(jnp.int32, (n, n), 0)
    col = lax.broadcasted_iota(jnp.int32, (n, n), 1)
    d = column(docs[...])
    same = jnp.concatenate([d, d], axis=1) == docs[...]
    visible = same & (row >= col)
    gains = gain[:, mine(width)].astype(F32)
    total = jnp.zeros((n, DH), F32)
    for h in range(width // DH):
        cols = slice(h * DH, (h + 1) * DH)
        scores = dot(q_out[:, cols], k_all[:, cols], ((1,), (1,)))
        weights = jnp.where(visible, scores, 0.0).astype(BF16)
        value = dot(weights, v_all[:, cols])
        intra[:, cols] = value
        total += value * value
        gate = jax.nn.sigmoid(g_all[:, cols].astype(F32))
        gate_out[:, cols] = gate * gains[:, cols]
    squares[...] = lane_sums(total)


def mixed_kernel(intra, q, t_near, t_far, docs, mixed, squares):
    n, width = q.shape
    tb = n // 2
    seen = column(docs[...]) == message_docs(t_near, chip() >= 1)[2]
    both = spanning(t_near, t_far, docs)
    total = jnp.zeros((n, DH), F32)
    for h in range(width // DH):
        cols = slice(h * DH, (h + 1) * DH)
        value = intra[:, cols] + jnp.where(seen, dot(q[:, cols], t_near[:DH, cols]), 0.0)
        first = jnp.where(both, dot(q[:tb, cols], t_far[:DH, cols]), 0.0)
        value = jnp.concatenate([value[:tb] + first, value[tb:]], axis=0)
        mixed[:, cols] = value
        total += value * value
    squares[...] = lane_sums(total)


def spanning(t_near, t_far, docs):
    near = message_docs(t_near, chip() >= 1)[2]
    far = message_docs(t_far, chip() >= 2)[2]
    return (column(docs[:, : docs.shape[1] // 2]) == near) & (near == far)


def normed(columns, mixed, gate, sums, out):
    scale = column(lax.rsqrt(sum(x[...] for x in sums) / columns + 1e-05))
    for h in range(mixed.shape[1] // DH):
        cols = slice(h * DH, (h + 1) * DH)
        out[:, cols] = (mixed[:, cols] * scale * gate[:, cols]).astype(BF16)


def norm_kernel(columns, mixed, gate, s0, s1, s2, out):
    normed(columns, mixed, gate, (s0, s1, s2), out)


def output_kernel(columns, mixed, gate, s0, s1, s2, out, kept, sent):
    tb = kept.shape[0]
    normed(columns, mixed, gate, (s0, s1, s2), out)
    kept[...], sent[...] = in_order(out[:tb, :], out[tb:, :])


def softmax_part(q, k, visible):
    scores = dot(q, k, ((1,), (1,))) * (1.0 / math.sqrt(DH))
    scores = jnp.where(visible, scores, NONE)
    top = jnp.max(scores, axis=1, keepdims=True)
    e = jnp.where(visible, jnp.exp(scores - top), 0.0)
    total = jnp.sum(e, axis=1, keepdims=True)
    some = jnp.where(total > 0.0, total, 1.0)
    return (e / some).astype(BF16), jnp.where(total > 0.0, top + jnp.log(some), NONE)


def pick_kernel(first, second, out):
    out[...] = jnp.where(inner() == 0, first[...], second[...])


def far_kernel(own, got, k_own, k_got, t_near, docs, weights, lse, k_all):
    tb, width = k_own.shape[0], k_all.shape[1]
    n = 2 * tb
    cols = mine(width)
    k_all[:tb, :], queries = in_order(own[:, cols], got[:, cols])
    place(k_all.at[tb:], k_own, k_got)
    near = message_docs(t_near, chip() >= 1)
    last = docs[:, n - 1 :]
    key_docs = jnp.concatenate([near[1], docs[...]], axis=1)
    visible = jnp.broadcast_to((key_docs == last) & (near[2] == last), (tb, 3 * tb))
    for h in range(width // DH):
        cols = slice(h * DH, (h + 1) * DH)
        weights[h], top = softmax_part(queries[:, cols], k_all[:, cols], visible)
        lse[:, cols] = as_row(top)


def answer_kernel(weights, lse, near_values, values, out):
    n, width = values.shape
    tb = n // 2
    for h in range(width // DH):
        cols = slice(h * DH, (h + 1) * DH)
        total = dot(weights[h, :, :tb], near_values[tb:, cols])
        total += dot(weights[h, :, tb:], values[:, cols])
        out[:tb, cols] = total.astype(BF16)
    high, middle, low = split(lse[...])
    rows = [high, middle, low, jnp.zeros((PAD - 3, width), BF16)]
    out[tb:, :] = jnp.concatenate([r.astype(F32) for r in rows], axis=0).astype(BF16)


def weights_kernel(
    q_own, k_own, q_got, k_got, near_first, near_first_got, near_last, near_last_got,
    t_near, docs, weights, first_weights, first_lse, q_all, k_all,
):
    n, width = q_all.shape
    tb = n // 2
    keys = 2 * n
    place(q_all, q_own, q_got)
    cols = mine(width)
    k_all[:tb, :] = in_order(near_first[:, cols], near_first_got[:, cols])[0]
    k_all[tb:n, :] = in_order(near_last[:, cols], near_last_got[:, cols])[0]
    place(k_all.at[n:], k_own, k_got)
    near_docs = message_docs(t_near, chip() >= 1)
    key_docs = jnp.concatenate([near_docs[0], near_docs[1], docs[...]], axis=1)
    d = column(docs[...])
    same = jnp.concatenate([d] * (keys // 128), axis=1) == key_docs
    row = lax.broadcasted_iota(jnp.int32, (n, keys), 0)
    col = lax.broadcasted_iota(jnp.int32, (n, keys), 1) - n
    visible = same & (row >= col)
    for h in range(width // DH):
        cols = slice(h * DH, (h + 1) * DH)
        weights[h], _ = softmax_part(q_all[:, cols], k_all[:, cols], visible)
        block = slice(n, n + tb)
        first_weights[h], top = softmax_part(
            q_all[:tb, cols], k_all[block, cols], visible[:tb, block]
        )
        first_lse[:, cols] = as_row(top)


def attend_kernel(weights, near, values, kept, sent):
    n, width = values.shape
    tb = n // 2
    top = inner() == 0
    for h in range(width // DH):
        cols = slice(h * DH, (h + 1) * DH)
        total = dot(weights[h, :, :n], near[:, cols])
        total += dot(weights[h, :, n:], values[:, cols])
        first, last = total[:tb].astype(BF16), total[tb:].astype(BF16)
        kept[:, cols] = jnp.where(top, first, last)
        sent[:, cols] = jnp.where(top, last, first)


def merge_kernel(
    weights, lse, values, answer, t_near, t_far, docs, kept, sent, new_kept, new_sent
):
    tb, width = kept.shape
    asked = spanning(t_near, t_far, docs)
    top_block = inner() == 0
    for h in range(width // DH):
        cols = slice(h * DH, (h + 1) * DH)
        far_lse = sum(answer[tb + i : tb + i + 1, cols].astype(F32) for i in range(3))
        top = jnp.maximum(far_lse, lse[:, cols])
        far, here = jnp.exp(far_lse - top), jnp.exp(lse[:, cols] - top)
        far, here = column(far / (far + here)), column(here / (far + here))
        merged = here * dot(weights[h], values[:tb, cols]) + far * answer[:tb, cols].astype(F32)
        before, other = in_order(kept[:, cols], sent[:, cols])
        rows = jnp.where(asked, merged.astype(BF16), before)
        new_kept[:, cols] = jnp.where(top_block, rows, other)
        new_sent[:, cols] = jnp.where(top_block, other, rows)


def join_kernel(kept, got, out):
    width = kept.shape[1]
    out[:, pl.ds(pl.multiple_of(inner() * width, DH), width)] = kept[...]
    out[:, pl.ds(pl.multiple_of((1 - inner()) * width, DH), width)] = got[...]


def run(kernel, ins, outs, scratch=(), us=0.5):
    got = pl.pallas_call(
        kernel,
        out_shape=[jax.ShapeDtypeStruct(*o) for o in outs],
        in_specs=[pl.BlockSpec(memory_space=pltpu.VMEM)] * len(ins),
        out_specs=[pl.BlockSpec(memory_space=pltpu.VMEM)] * len(outs),
        scratch_shapes=scratch,
        compiler_params=pltpu.CompilerParams(vmem_limit_bytes=VMEM_LIMIT),
        cost_estimate=pl.CostEstimate(
            flops=0, bytes_accessed=int(us * BYTES_PER_US), transcendentals=0
        ),
    )(*ins)
    return got[0] if len(got) == 1 else got


def swap(x):
    return lax.ppermute(x, "inner", [(0, 1), (1, 0)])


def next_chip(x, line=False):
    chips = lax.axis_size("outer")
    if line:
        return lax.ppermute(x, "outer", [(i, i + 1) for i in range(chips - 1)])
    return lax.ppermute(x, "outer", [(i, (i + 1) % chips) for i in range(chips)])


def both_ways(x):
    last = lax.axis_size("outer") - 1
    up = [(2 * i, 2 * i + 2) for i in range(last)] + [(2 * last, 2 * last + 1)]
    down = [(2 * i + 1, 2 * i - 1) for i in range(1, last + 1)] + [(1, 0)]
    return lax.ppermute(x, ("outer", "inner"), up + down)


def other_heads(x):
    size = lax.axis_size("heads")
    if size != 4:
        return [lax.psum(x, "heads") - x, jnp.zeros_like(x)]
    one = lax.ppermute(x, "heads", [(i, i ^ 1) for i in range(size)])
    return [one, lax.ppermute(x + one, "heads", [(i, i ^ 2) for i in range(size)])]


def over_heads(x):
    x = x + swap(x)
    return [x, *other_heads(x)]


def per_device(
    lin_query, lin_key, lin_value, gate_input, norm_gain, segment_ids, soft_query, soft_key
):
    tb, local = lin_query.shape
    width = local // 2
    n = 2 * tb
    heads = width // DH
    columns = local * lax.axis_size("heads")
    block, whole = ((tb, width), BF16), ((n, width), BF16)
    scratch = pltpu.VMEM((n, width), BF16)
    tie = lax.optimization_barrier

    def joined(kept, sent):
        return run(join_kernel, [kept, swap(sent)], [((tb, local), BF16)])

    own_docs = segment_ids[None]
    got_docs = swap(own_docs)
    lk_got, lv_got = swap(lin_key), swap(lin_value)
    keys, values, own_docs = run(
        cut_kernel, [lin_key, lin_value, own_docs], [block, block, ((1, tb), F32)], us=2.0
    )
    t_msg, docs = run(
        state_kernel,
        [keys, values, lk_got, lv_got, own_docs, got_docs],
        [((DH + PAD, width), BF16), ((1, n), F32)],
    )
    t_near = next_chip(t_msg)
    raw_key = soft_key
    lin_query, gate_input, soft_query, soft_key, _ = tie(
        (lin_query, gate_input, soft_query, soft_key, t_msg)
    )
    lq_got, g_got = swap(lin_query), swap(gate_input)
    sq_got, sk_got = swap(soft_query), swap(soft_key)
    intra, queries, gate, squares = run(
        intra_kernel,
        [
            lin_query, keys, values, gate_input, lq_got, lk_got, lv_got, g_got,
            norm_gain[None], docs,
        ],
        [((n, width), F32), whole, ((n, width), F32), ((1, n), F32)],
        [scratch] * 3,
        us=1.2,
    )
    chip_squares = squares + swap(squares)
    sums = [chip_squares, *other_heads(chip_squares)]
    t_far = next_chip(t_near, line=True)
    sums, t_far = tie((sums, t_far))
    early = run(functools.partial(norm_kernel, columns), [intra, gate, *sums], [whole], us=0.3)
    first_own = both_ways(tie((raw_key, t_msg))[0])
    out_last = run(pick_kernel, [sk_got, sq_got], [((tb, local), BF16)], us=0.3)
    last_own = both_ways(tie((out_last, chip_squares))[0])
    near_values = next_chip(early, line=True)
    mixed, squares = run(
        mixed_kernel, [intra, queries, t_near, t_far, docs], [((n, width), F32), ((1, n), F32)]
    )
    values, lin_kept, lin_sent = run(
        functools.partial(output_kernel, columns),
        [mixed, gate, *over_heads(squares)],
        [whole, block, block],
        us=0.3,
    )
    first_got, last_got = swap(first_own), swap(last_own)
    far_weights, far_lse = run(
        far_kernel,
        [last_own, last_got, soft_key, sk_got, t_near, docs],
        [((heads, tb, 3 * tb), BF16), ((1, width), F32)],
        [pltpu.VMEM((3 * tb, width), BF16)],
        us=1.0,
    )
    far_weights, near_values = tie((far_weights, near_values))
    weights, first_weights, first_lse = run(
        weights_kernel,
        [
            soft_query, soft_key, sq_got, sk_got, first_own, first_got, last_own, last_got,
            t_near, docs,
        ],
        [((heads, n, 2 * n), BF16), ((heads, tb, tb), BF16), ((1, width), F32)],
        [scratch, pltpu.VMEM((2 * n, width), BF16)],
        us=2.5,
    )
    values, near_values = tie((values, near_values))
    answer = next_chip(
        run(
            answer_kernel,
            [far_weights, far_lse, near_values, values],
            [((tb + PAD, width), BF16)],
            us=0.3,
        ),
        line=True,
    )
    linear_out = joined(lin_kept, lin_sent)
    kept, sent = run(attend_kernel, [weights, near_values, values], [block, block], us=0.8)
    kept, sent = run(
        merge_kernel,
        [first_weights, first_lse, values, answer, t_near, t_far, docs, kept, sent],
        [block, block],
    )
    return linear_out, joined(kept, sent)


def solution(mesh):
    tokens = P(("outer", "inner"), "heads")
    return jax.shard_map(
        per_device,
        mesh=mesh,
        in_specs=(tokens, tokens, tokens, tokens, P("heads"), P(("outer", "inner")), tokens, tokens),
        out_specs=(tokens, tokens),
        check_vma=False,
    )
```
